32 devices in a mesh: ctx: 8 (over y, x, core), tp: 4 (over z).
Axes of the slice: x: 2, y: 2, z: 4, core: 2. Of those that a mesh axis runs over, the one named last changes fastest.
Arguments:
- query_rows: bfloat16 [4096, 8192], P('ctx', 'tp'), may hold values from -6 to 6
- key_rows: bfloat16 [4096, 8192], P('ctx', 'tp'), may hold values from -6 to 6
- value_rows: bfloat16 [4096, 8192], P('ctx', 'tp'), may hold values from -6 to 6
- positions: int32 [8, 512], replicated, may hold values from -1 to 255, as said below
- filters: float32 [8192, 2048], P(('tp', 'ctx')), may hold values from -6 to 6
- bias_term: float32 [8192], P(('tp', 'ctx')), may hold values from -4 to 4
- grad_out: bfloat16 [2048, 8192], P(('ctx', 'tp')), may hold values from -6 to 6
Outputs:
- output: bfloat16 [2048, 8192], P('ctx', 'tp')
- grad_query: bfloat16 [2048, 8192], P('ctx', 'tp')
- grad_key: bfloat16 [2048, 8192], P('ctx', 'tp')
- grad_value: bfloat16 [2048, 8192], P('ctx', 'tp')
- grad_filters: float32 [8192, 2048], P(('tp', 'ctx'))
The draws below stay inside these ranges and needn't reach their ends.
Inputs may be any that keep to these rules, and one draw needn't show every extreme that they name: Entries j * 64 to (j + 1) * 64 - 1 of row i list the positions within context shard j of the rows that loader buffer i holds for shard j, or -1 for an unused row; live rows come first in such a slot and carry consecutive positions (one run of a segment). Over all buffers every position of every shard appears exactly once, and for every shard some buffer fills its whole slot of 64 rows.
All inputs are finite; a program needn't handle non-finite values.
Results may differ from the reference program's by a relative error of at most 0.0058.
Values may be sent and summed in bfloat16 or wider, within the bound.
No kernel may reach another device: no remote copies, remote signals or barrier semaphores. Data moves between devices by JAX's collectives and lax.ppermute only.
A program may use at most 128 MiB of HBM per device.

```python
import math
import jax
import jax.numpy as jnp
from jax import lax

D = 8192
TOK_DEV = 256
TOKENS = 2048
BUF = 512
SLOT = 64
N_CTX = 8


def draw_positions(key, part):
    shards = N_CTX
    slot_rows = SLOT
    key_order, key_split = jax.random.split(key)
    orders = jax.vmap(lambda subkey: jax.random.permutation(subkey, shards))(jax.random.split(key_order, shards))
    leading = jax.random.randint(key_split, (shards, shards // 2), 0, slot_rows + 1)
    leading = leading.at[:, 0].set(slot_rows)
    run_lengths = jnp.stack([leading, slot_rows - leading], axis=2).reshape(shards, shards)
    run_starts = jnp.cumsum(run_lengths, axis=1) - run_lengths
    place_of = jnp.zeros((shards, shards), jnp.int32).at[jnp.arange(shards)[:, None], orders].set(jnp.broadcast_to(jnp.arange(shards, dtype=jnp.int32)[None, :], (shards, shards)))
    held_rows = jnp.take_along_axis(run_lengths, place_of, axis=1)
    run_start = jnp.take_along_axis(run_starts, place_of, axis=1)
    offset = jnp.arange(slot_rows, dtype=jnp.int32)
    positions_table = jnp.where(offset[None, None, :] < held_rows[:, :, None], run_start[:, :, None] + offset[None, None, :], -1)
    return jnp.transpose(positions_table, (1, 0, 2)).reshape(shards, shards * slot_rows).astype(jnp.int32)


def block_scale(rng, shape, cuts, low, largest):
    def one(dim, blocks):
        steps = jax.random.uniform(jax.random.fold_in(jax.random.fold_in(rng, 6), dim), (blocks,), jnp.float32, low / len(cuts), largest / len(cuts))
        return jnp.repeat(jnp.exp(steps), shape[dim] // blocks).reshape((-1,) + (1,) * (len(shape) - dim - 1))

    loudness = one(*cuts[0])
    for cut in cuts[1:]:
        loudness = loudness * one(*cut)
    return loudness


def scatter_about(stream_key, dims, spread, most, cuts=(), held_as=jnp.bfloat16):
    values = jax.random.normal(stream_key, dims, jnp.float32) * spread
    if len(cuts) > 0:
        values = block_scale(stream_key, dims, cuts, -0.22, 0.18) * values
    return jnp.clip(values, min=-most, max=most).astype(held_as)


def setup_inputs(seed: int = 0) -> dict:
    streams_of = jax.random.split(jax.random.key(seed), 8)
    return {
        "query_rows": scatter_about(streams_of[0], (N_CTX * BUF, D), 1.0, 6.0, ((0, 8), (1, 4))),
        "key_rows": scatter_about(streams_of[1], (N_CTX * BUF, D), 1.0, 6.0, ((0, 8), (1, 4))),
        "value_rows": scatter_about(streams_of[2], (N_CTX * BUF, D), 1.0, 6.0, ((0, 8), (1, 4))),
        "positions": draw_positions(jax.random.fold_in(streams_of[7], 71), 0),
        "filters": scatter_about(streams_of[4], (D, TOKENS), 1.0, 6.0, ((0, 32),), jnp.float32),
        "bias_term": scatter_about(streams_of[5], (D,), 1.0, 4.0, ((0, 32),), jnp.float32),
        "grad_out": scatter_about(streams_of[6], (TOKENS, D), 1.0, 6.0, ((0, 32),)),
    }


def settle_rows(rows, positions):
    column = jnp.arange(positions.shape[1], dtype=jnp.int32) // SLOT
    target = jnp.where(positions >= 0, column[None, :] * TOK_DEV + positions, TOKENS)
    target = target.reshape(-1).astype(jnp.int32)
    empty = jnp.zeros((TOKENS, rows.shape[1]), rows.dtype)
    return empty.at[target].set(rows, mode='drop')

def channel_block(pieces):
    signal, grad_conv, filters, bias_term = pieces
    length = 2 * TOKENS
    factor = 1.0 / math.sqrt(TOKENS)
    spec_signal = jnp.fft.rfft(signal, n=length, axis=1)
    spec_filter = jnp.fft.rfft(filters, n=length, axis=1)
    spec_grad = jnp.fft.rfft(grad_conv, n=length, axis=1)
    forward_conv = jnp.fft.irfft(spec_filter * spec_signal, n=length, axis=1)[:, :TOKENS]
    backward_conv = jnp.fft.irfft(jnp.conj(spec_filter) * spec_grad, n=length, axis=1)[:, :TOKENS]
    filter_corr = jnp.fft.irfft(jnp.conj(spec_signal) * spec_grad, n=length, axis=1)[:, :TOKENS]
    conv_out = bias_term[:, None] * signal + factor * forward_conv
    grad_signal = bias_term[:, None] * grad_conv + factor * backward_conv
    return (conv_out, grad_signal, factor * filter_corr)

def reference(query_rows, key_rows, value_rows, positions, filters, bias_term, grad_out):
    query_seq = settle_rows(query_rows, positions)
    key_seq = settle_rows(key_rows, positions)
    value_seq = settle_rows(value_rows, positions)
    signal = (key_seq.astype(jnp.float32) * value_seq.astype(jnp.float32)).astype(jnp.bfloat16)
    grad_conv = (grad_out.astype(jnp.float32) * query_seq.astype(jnp.float32)).astype(jnp.bfloat16)
    width_block = min(256, D)
    blocks_count = D // width_block

    def stacked(array):
        return array.astype(jnp.float32).T.reshape(blocks_count, width_block, TOKENS)
    conv_out, grad_signal, grad_filters = lax.map(channel_block, (stacked(signal), stacked(grad_conv), filters.reshape(blocks_count, width_block, TOKENS), bias_term.reshape(blocks_count, width_block)))
    conv_out = conv_out.reshape(D, TOKENS).T.astype(jnp.bfloat16)
    grad_signal = grad_signal.reshape(D, TOKENS).T.astype(jnp.bfloat16)
    grad_filters = grad_filters.reshape(D, TOKENS)
    output = (query_seq.astype(jnp.float32) * conv_out.astype(jnp.float32)).astype(jnp.bfloat16)
    grad_query = (grad_out.astype(jnp.float32) * conv_out.astype(jnp.float32)).astype(jnp.bfloat16)
    grad_key = (grad_signal.astype(jnp.float32) * value_seq.astype(jnp.float32)).astype(jnp.bfloat16)
    grad_value = (grad_signal.astype(jnp.float32) * key_seq.astype(jnp.float32)).astype(jnp.bfloat16)
    return (output, grad_query, grad_key, grad_value, grad_filters)
```

```python
import functools
import math

import jax
import jax.numpy as jnp
import ml_dtypes
import numpy as np
from jax import lax
from jax.experimental import pallas as pl
from jax.experimental.pallas import tpu as pltpu
from jax.sharding import PartitionSpec as P

F32 = jnp.float32
BF16 = jnp.bfloat16
ROWS = 16
VMEM_LIMIT = 63_000_000


@functools.lru_cache(maxsize=None)
def dense_tables(shards, span):
    points = 2 * shards * span
    half = span // 2
    r = np.arange(span)
    forward = np.zeros((shards, 2 * span, 2 * span))
    for k1 in range(1, shards):
        bins = k1 + 2 * shards * np.arange(span)
        angle = (bins[:, None] * r[None, :] % points) * (2.0 * np.pi / points)
        cos, sin = np.cos(angle), np.sin(angle)
        forward[k1] = np.block([[cos, sin], [-sin, cos]])
    for place, k1 in ((0, 0), (1, shards)):
        bins = k1 + 2 * shards * np.arange(half)
        angle = (bins[:, None] * r[None, :] % points) * (2.0 * np.pi / points)
        columns = slice(place * span, place * span + span)
        forward[0, place * half : place * half + half, columns] = np.cos(angle)
        forward[0, span + place * half : span + place * half + half, columns] = -np.sin(angle)
    forward[0, span, :span] = 1.0 - 2.0 * (r % 2)
    inverse = 2.0 * np.transpose(forward, (0, 2, 1))
    inverse[0, :, 0] *= 0.5
    inverse[0, :, span] *= 0.5

    def parts(table):
        table = table.astype(np.float32)
        high = table.astype(ml_dtypes.bfloat16)
        low = (table - high.astype(np.float32)).astype(ml_dtypes.bfloat16)
        return high, low

    return parts(forward), parts(inverse)


def plus(a, b):
    if a is None:
        return b
    return a if b is None else a + b


def minus(a, b):
    if b is None:
        return a
    return -b if a is None else a - b


def turned(z, step, count, sign):
    angle = sign * 2.0 * math.pi * (step % count) / count
    cos, sin = math.cos(angle), math.sin(angle)
    re, im = z
    if abs(sin) < 1e-9:
        return z if cos > 0 else (minus(None, re), minus(None, im))
    if abs(cos) < 1e-9:
        return (minus(None, im), re) if sin > 0 else (im, minus(None, re))
    if re is None and im is None:
        return z
    if im is None:
        return (re * cos, re * sin)
    if re is None:
        return (im * -sin, im * cos)
    if abs(abs(cos) - abs(sin)) < 1e-9:
        root = math.sqrt(0.5)
        first = re - im if sin * cos > 0 else re + im
        second = re + im if sin * cos > 0 else im - re
        c = root if cos > 0 else -root
        return (first * c, second * c)
    return (re * cos - im * sin, im * cos + re * sin)


def spread(values, sign):
    count = len(values)
    if count == 1:
        return values
    half = count // 2
    low, high = values[:half], values[half:]
    even = [(plus(a[0], b[0]), plus(a[1], b[1])) for a, b in zip(low, high)]
    odd = [
        turned((minus(a[0], b[0]), minus(a[1], b[1])), step, count, sign)
        for step, (a, b) in enumerate(zip(low, high))
    ]
    out = [None] * count
    out[0::2] = spread(even, sign)
    out[1::2] = spread(odd, sign)
    return out


def gather_up(values, sign):
    count = len(values)
    if count == 1:
        return values
    half = count // 2
    even = gather_up(values[0::2], sign)
    odd = [turned(z, step, count, sign) for step, z in enumerate(gather_up(values[1::2], sign))]
    return [(plus(a[0], b[0]), plus(a[1], b[1])) for a, b in zip(even, odd)] + [
        (minus(a[0], b[0]), minus(a[1], b[1])) for a, b in zip(even, odd)
    ]


def dot(a, b):
    return jnp.dot(a, b, preferred_element_type=F32)


def shard_transform(load, high_ref, low_ref=None):
    shards, rows, width = high_ref.shape
    span = rows // 2
    lanes = min(128, width)

    def body(step, carry):
        first = pl.multiple_of(step * ROWS, ROWS)
        for lane in range(0, width, lanes):
            values = [(load(i, pl.ds(first, ROWS), pl.ds(lane, lanes)), None) for i in range(shards)]
            values = spread(values + [(None, None)] * shards, -1)
            for k1 in range(shards):
                pair = (values[0][0], values[shards][0]) if k1 == 0 else values[k1]
                for part, value in enumerate(pair):
                    where = pl.ds(pl.multiple_of(part * span + first, ROWS), ROWS)
                    high = value.astype(BF16)
                    high_ref[k1, where, pl.ds(lane, lanes)] = high
                    if low_ref is not None:
                        low = (value - high.astype(F32)).astype(BF16)
                        low_ref[k1, where, pl.ds(lane, lanes)] = low
        return carry

    lax.fori_loop(0, span // ROWS, body, 0)


def shard_inverse(slab_ref, store):
    shards, rows, width = slab_ref.shape
    span = rows // 2
    lanes = min(128, width)

    def body(step, carry):
        first = pl.multiple_of(step * ROWS, ROWS)
        for lane in range(0, width, lanes):
            def load(k1, part):
                where = pl.ds(pl.multiple_of(part * span + first, ROWS), ROWS)
                return slab_ref[k1, where, pl.ds(lane, lanes)]

            values = [(load(0, 0), None)]
            values += [(load(k1, 0), load(k1, 1)) for k1 in range(1, shards)]
            values += [(load(0, 1), None)] + [(None, None)] * (shards - 1)
            values = gather_up(values, 1)
            for i in range(shards):
                store(i, pl.ds(first, ROWS), pl.ds(lane, lanes), values[i][0])
        return carry

    lax.fori_loop(0, span // ROWS, body, 0)


def bin_product(a, b, conjugate, first_slab):
    span = a.shape[0] // 2
    ar, ai, br, bi = a[:span], a[span:], b[:span], b[span:]
    cross = ai * bi
    shared = cross
    im = ai * br - ar * bi if conjugate else ar * bi + ai * br
    if first_slab is not False:
        alone = (lax.broadcasted_iota(jnp.int32, (span, 1), 0) == 0) & first_slab
        shared = jnp.where(alone, 0.0, cross)
        im = jnp.where(alone, cross, im)
    re = ar * br + shared if conjugate else ar * br - shared
    return jnp.concatenate([re.astype(BF16), im.astype(BF16)], axis=0)


def filter_kernel(filters_ref, fh_ref, fl_ref, after_ref, spec_ref, seq_ref, high_ref, low_ref):
    slab = pl.program_id(0)
    shards, span = seq_ref.shape[:2]

    @pl.when(slab == 0)
    def _():
        for i in range(shards):
            seq_ref[i] = filters_ref[:, i * span : (i + 1) * span].T
        shard_transform(lambda i, r, c: seq_ref[i, r, c], high_ref, low_ref)

    high = high_ref[slab]
    spec_ref[0] = dot(fh_ref[0], high) + dot(fh_ref[0], low_ref[slab]) + dot(fl_ref[0], high)


def conv_kernel(conjugate, scale, n_in, turn_ref, *refs):
    pieces, refs = refs[:n_in], refs[n_in:]
    bias_ref, other_hbm, fh_hbm, ih_hbm, after_ref, out_ref, spec_hbm = refs[:7]
    fh_ref, ih_ref, other_ref, spec_ref, high_ref, slab_ref, in_sems, out_sems = refs[7:15]
    seq_ref = pieces[0] if n_in == 1 else refs[15]
    shards = fh_ref.shape[0]

    def fetch(which, slab):
        source, target = ((fh_hbm, fh_ref), (other_hbm, other_ref), (ih_hbm, ih_ref))[which]
        return pltpu.make_async_copy(source.at[slab], target.at[slab], in_sems.at[which, slab])

    def keep(slab):
        return pltpu.make_async_copy(spec_ref.at[slab], spec_hbm.at[slab], out_sems.at[slab])

    for slab in range(shards):
        for which in range(3):
            fetch(which, slab).start()
    if n_in > 1:
        for number in range(n_in):
            seq_ref[turn_ref[0] ^ number] = pieces[number][...]

    def load(i, rows, lanes):
        return seq_ref[i, rows, lanes].astype(F32)

    shard_transform(load, high_ref)

    def forward(slab):
        fetch(0, slab).wait()
        spec_ref[slab] = dot(fh_ref[slab], high_ref[slab])
        keep(slab).start()

    forward(0)
    for slab in range(shards):
        if slab + 1 < shards:
            forward(slab + 1)
        fetch(1, slab).wait()
        product = bin_product(spec_ref[slab], other_ref[slab], conjugate, slab == 0)
        fetch(2, slab).wait()
        slab_ref[slab] = dot(ih_ref[slab], product)

    def store(i, rows, lanes, value):
        direct = bias_ref[:, lanes] * load(i, rows, lanes)
        out_ref[i, rows, lanes] = (direct + scale * value).astype(BF16)

    shard_inverse(slab_ref, store)
    for slab in range(shards):
        keep(slab).wait()


def correlation_kernel(scale, spec_ref, other_ref, ih_ref, out_ref, slab_ref, seq_ref):
    slab = pl.program_id(0)
    shards = pl.num_programs(0)
    span = seq_ref.shape[1]
    slab_ref[slab] = dot(ih_ref[0], bin_product(spec_ref[0], other_ref[0], True, slab == 0))

    @pl.when(slab == shards - 1)
    def _():
        def store(i, rows, lanes, value):
            seq_ref[i, rows, lanes] = scale * value

        shard_inverse(slab_ref, store)
        for i in range(seq_ref.shape[0]):
            out_ref[:, i * span : (i + 1) * span] = seq_ref[i].T


def placement(own_ref, select_ref):
    tokens, slots = select_ref.shape
    token = lax.broadcasted_iota(jnp.int32, (tokens, slots), 0)
    select_ref[...] = jnp.where(token == own_ref[...], 1.0, 0.0).astype(BF16)


def pack_kernel(shards, turn_ref, *refs):
    sources, outs = refs[: -shards - 3], refs[-shards - 3 : -3]
    held, in_sems, out_sems = refs[-3:]
    rows = sources[0].shape[0] // shards

    def read(number, place):
        start = pl.multiple_of((turn_ref[0] ^ number) * rows, rows)
        return pltpu.make_async_copy(
            sources[place].at[pl.ds(start, rows)],
            held.at[number, pl.ds(place * rows, rows)],
            in_sems.at[number, place],
        )

    def write(number):
        return pltpu.make_async_copy(held.at[number], outs[number], out_sems.at[number])

    for number in range(shards):
        for place in range(len(sources)):
            read(number, place).start()
    for number in range(shards):
        for place in range(len(sources)):
            read(number, place).wait()
        write(number).start()
    for number in range(shards):
        write(number).wait()


def by_owner(turn, outs, value_ref):
    width = outs[0].shape[-1]
    parts = value_ref.shape[1] // width
    if len(outs) == 1:
        for part in range(parts):
            outs[0][part] = value_ref[:, part * width : (part + 1) * width]
        return
    for step in range(len(outs) // parts):

        @pl.when(pl.program_id(0) == step)
        def _(step=step):
            for part in range(parts):
                lanes = pl.ds(pl.multiple_of(((turn % parts) ^ part) * width, width), width)
                outs[step * parts + part][...] = value_ref[:, lanes]


def gate_kernel(*refs):
    pass


def settle_signal_kernel(shards, turn_ref, own_ref, after_ref, *refs):
    slots, (key_out, value_out), outs = refs[:shards], refs[shards : shards + 2], refs[shards + 2 : -2]
    select_ref, product_ref = refs[-2:]

    @pl.when(pl.program_id(0) == 0)
    def _():
        placement(own_ref, select_ref)

    slot_rows = slots[0].shape[0] // 2
    key = dot(select_ref[...], jnp.concatenate([slot[:slot_rows] for slot in slots], axis=0))
    value = dot(select_ref[...], jnp.concatenate([slot[slot_rows:] for slot in slots], axis=0))
    key_out[...] = key.astype(BF16)
    value_out[...] = value.astype(BF16)
    product_ref[...] = (key * value).astype(BF16)
    by_owner(turn_ref[0], outs, product_ref)


def settle_query_kernel(tensor, source_ref, own_ref, rows_ref, *refs):
    pieces = refs[:tensor]
    grad_out, query_out, out_ref, select_ref, product_ref = refs[-5:]

    @pl.when(pl.program_id(0) == 0)
    def _():
        placement(own_ref, select_ref)

    rows = pieces[0].shape[0]
    for number, piece in enumerate(pieces):
        start = pl.multiple_of(source_ref[number] * rows, rows)
        grad_out[pl.ds(start, rows), :] = piece[...]
    query = dot(select_ref[...], rows_ref[...])
    query_out[...] = query.astype(BF16)
    product_ref[...] = (query * grad_out[...].astype(F32)).astype(BF16)
    by_owner(None, [out_ref], product_ref)


def final_kernel(shared_ref, a_ref, b_ref, after_ref, a_out, b_out):
    width = shared_ref.shape[2]
    for part in range(shared_ref.shape[0]):
        lanes = slice(part * width, (part + 1) * width)
        shared = shared_ref[part].astype(F32)
        a_out[:, lanes] = (a_ref[:, lanes].astype(F32) * shared).astype(BF16)
        b_out[:, lanes] = (b_ref[:, lanes].astype(F32) * shared).astype(BF16)


def cost(flops, moved):
    return pl.CostEstimate(flops=int(flops), bytes_accessed=int(moved), transcendentals=0)


def params():
    return pltpu.CompilerParams(
        dimension_semantics=("arbitrary",), vmem_limit_bytes=VMEM_LIMIT
    )


def whole(shape):
    return pl.BlockSpec(shape, lambda j, *turn: (0,) * len(shape))


def slab_of(shape):
    return pl.BlockSpec((1,) + shape[1:], lambda j, *turn: (j, 0, 0))


UNREAD = pl.BlockSpec(memory_space=pl.ANY)


def shape_of(shape, dtype):
    return jax.ShapeDtypeStruct(shape, dtype)


def filter_spectrum(filters, tables, after):
    (fh, fl), _ = tables
    width, length = filters.shape
    shards, rows, _ = fh.shape
    spec = (shards, rows, width)
    return pl.pallas_call(
        filter_kernel,
        grid=(shards,),
        in_specs=[whole(filters.shape), slab_of(fh.shape), slab_of(fl.shape), UNREAD],
        out_specs=slab_of(spec),
        out_shape=shape_of(spec, F32),
        scratch_shapes=[
            pltpu.VMEM((shards, rows // 2, width), F32),
            pltpu.VMEM(spec, BF16),
            pltpu.VMEM(spec, BF16),
        ],
        compiler_params=params(),
        cost_estimate=cost(6 * shards * rows * rows * width, 4 * filters.size + 8 * fh.size),
        name="filter_spectrum",
    )(filters, fh, fl, after)


def convolve(turn, pieces, bias, other, tables, conjugate, after):
    (fh, _), (ih, _) = tables
    shards, rows, _ = fh.shape
    tokens, width = pieces[0].shape[-2:]
    spec = (shards, rows, width)
    seq = (shards, tokens, width)
    length = shards * tokens
    scale = 1.0 / (2 * length * math.sqrt(length))
    return pl.pallas_call(
        functools.partial(conv_kernel, conjugate, scale, len(pieces)),
        grid_spec=pltpu.PrefetchScalarGridSpec(
            num_scalar_prefetch=1,
            grid=(1,),
            in_specs=[whole(piece.shape) for piece in pieces] + [whole(bias.shape)] + [UNREAD] * 4,
            out_specs=[whole(seq), UNREAD],
            scratch_shapes=[
                pltpu.VMEM(fh.shape, BF16),
                pltpu.VMEM(ih.shape, BF16),
                pltpu.VMEM(spec, F32),
                pltpu.VMEM(spec, F32),
                pltpu.VMEM(spec, BF16),
                pltpu.VMEM(spec, F32),
                pltpu.SemaphoreType.DMA((3, shards)),
                pltpu.SemaphoreType.DMA((shards,)),
            ]
            + [pltpu.VMEM(seq, BF16)] * (len(pieces) > 1),
        ),
        out_shape=[shape_of(seq, BF16), shape_of(spec, F32)],
        compiler_params=params(),
        cost_estimate=cost(4 * shards * rows * rows * width, 4 * fh.size + 12 * shards * rows * width),
        name="convolve_backward" if conjugate else "convolve_forward",
    )(turn, *pieces, bias, other, fh, ih, after)


def correlate(spec_a, spec_b, tables):
    _, (ih, _) = tables
    shards, rows, width = spec_a.shape
    length = shards * rows // 2
    scale = 1.0 / (2 * length * math.sqrt(length))
    return pl.pallas_call(
        functools.partial(correlation_kernel, scale),
        grid=(shards,),
        in_specs=[slab_of(spec_a.shape), slab_of(spec_b.shape), slab_of(ih.shape)],
        out_specs=whole((width, length)),
        out_shape=shape_of((width, length), F32),
        scratch_shapes=[
            pltpu.VMEM(spec_a.shape, F32),
            pltpu.VMEM((shards, rows // 2, width), F32),
        ],
        compiler_params=params(),
        cost_estimate=cost(4 * shards * rows * rows * width, 2 * ih.size + 12 * spec_a.size),
        name="filter_gradient",
    )(spec_a, spec_b, ih)


def pack(turn, arrays, shards):
    rows, channels = arrays[0].shape
    rows = len(arrays) * rows // shards
    moved = 4 * len(arrays) * arrays[0].size
    return pl.pallas_call(
        functools.partial(pack_kernel, shards),
        grid_spec=pltpu.PrefetchScalarGridSpec(
            num_scalar_prefetch=1,
            grid=(1,),
            in_specs=[pl.BlockSpec(memory_space=pl.ANY)] * len(arrays),
            out_specs=[pl.BlockSpec(memory_space=pl.ANY)] * shards,
            scratch_shapes=[
                pltpu.VMEM((shards, rows, channels), arrays[0].dtype),
                pltpu.SemaphoreType.DMA((shards, len(arrays))),
                pltpu.SemaphoreType.DMA((shards,)),
            ],
        ),
        out_shape=[shape_of((rows, channels), arrays[0].dtype)] * shards,
        compiler_params=params(),
        cost_estimate=cost(0, moved),
        name="pack_rows",
    )(turn, *arrays)


def column_plan(channels, shards, lanes):
    width = channels // shards
    parts = min(shards, max(1, lanes // width))
    return width, parts, parts * width, shards // parts


def column(rows, block):
    return pl.BlockSpec((rows, block), lambda j: (0, j))


def turned_column(rows, block, parts, pieces):
    if pieces:
        return pl.BlockSpec((rows, block), lambda j, turn: (0, j ^ (turn[0] // parts)))
    return pl.BlockSpec((rows, block), lambda j, turn: (0, j))


def gate(value, after):
    return pl.pallas_call(
        gate_kernel,
        in_specs=[UNREAD] * (1 + len(after)),
        out_specs=UNREAD,
        out_shape=shape_of(value.shape, value.dtype),
        input_output_aliases={0: 0},
        name="gate",
    )(value, *after)


def settle_signal(turn, own, slots, tokens, n_out, after):
    shards = len(slots)
    slot_rows, channels = slots[0].shape
    count = shards * slot_rows // 2
    width, parts, block, steps = column_plan(channels, shards, 512)
    seq = shape_of((tokens, channels), BF16)
    column_at = functools.partial(turned_column, block=block, parts=parts, pieces=n_out > 1)
    if n_out > 1:
        out_spec, out_shape = whole((tokens, width)), shape_of((tokens, width), BF16)
    else:
        out_spec = pl.BlockSpec((parts, tokens, width), lambda j, turn: (j, 0, 0))
        out_shape = shape_of((shards, tokens, width), BF16)
    outs = pl.pallas_call(
        functools.partial(settle_signal_kernel, shards),
        grid_spec=pltpu.PrefetchScalarGridSpec(
            num_scalar_prefetch=1,
            grid=(steps,),
            in_specs=[whole(own.shape), UNREAD] + [column_at(slot_rows)] * shards,
            out_specs=[column_at(tokens)] * 2 + [out_spec] * n_out,
            scratch_shapes=[pltpu.VMEM((tokens, count), BF16), pltpu.VMEM((tokens, block), BF16)],
        ),
        out_shape=[seq, seq] + [out_shape] * n_out,
        compiler_params=params(),
        cost_estimate=cost(4 * tokens * count * channels, 4 * count * channels + 6 * tokens * channels),
        name="settle_signal",
    )(turn, own, after, *slots)
    return outs[0], outs[1], outs[2:]


def settle_query(own, rows, sources, pieces, tokens, shards, after):
    count, channels = rows.shape
    width, parts, block, steps = column_plan(channels, shards, 512)
    seq = shape_of((tokens, channels), BF16)
    return pl.pallas_call(
        functools.partial(settle_query_kernel, len(pieces)),
        grid=(steps,),
        in_specs=[pl.BlockSpec(memory_space=pltpu.SMEM), whole(own.shape), column(count, block)]
        + [column(piece.shape[0], block) for piece in pieces]
        + [UNREAD] * len(after),
        out_specs=[column(tokens, block)] * 2
        + [pl.BlockSpec((parts, tokens, width), lambda j: (j, 0, 0))],
        out_shape=[seq, seq, shape_of((shards, tokens, width), BF16)],
        scratch_shapes=[pltpu.VMEM((tokens, count), BF16), pltpu.VMEM((tokens, block), BF16)],
        compiler_params=params(),
        cost_estimate=cost(2 * tokens * count * channels, 2 * count * channels + 8 * tokens * channels),
        name="settle_query",
    )(sources, own, rows, *pieces, *after)


def final_products(shared, a, b, after, name):
    shards, tokens, width = shared.shape
    _, parts, block, steps = column_plan(a.shape[1], shards, 1024)
    return pl.pallas_call(
        final_kernel,
        grid=(steps,),
        in_specs=[
            pl.BlockSpec((parts, tokens, width), lambda j: (j, 0, 0)),
            column(tokens, block), column(tokens, block), UNREAD,
        ],
        out_specs=[column(tokens, block)] * 2,
        out_shape=[shape_of(a.shape, BF16)] * 2,
        compiler_params=params(),
        cost_estimate=cost(2 * a.size, 10 * a.size),
        name=name,
    )(shared, a, b, after)


def permuted(pieces):
    shards = len(pieces)
    order = sorted(range(1, shards), key=lambda number: (number < 2, number & 1, number))
    received = {
        number: lax.ppermute(pieces[number], "ctx", [(i, i ^ number) for i in range(shards)])
        for number in order
    }
    return [pieces[0]] + [received[number] for number in range(1, shards)]


def exchange(value):
    return lax.all_to_all(value, "ctx", split_axis=0, concat_axis=0, tiled=True)


def per_device(query_rows, key_rows, value_rows, positions, filters, bias_term, grad_out):
    shards = lax.axis_size("ctx")
    ctx_index = lax.axis_index("ctx")
    slots, channels = query_rows.shape
    slot_rows = slots // shards
    tokens = filters.shape[1] // shards
    tables = dense_tables(shards, tokens)

    tensor = lax.axis_size("tp")
    tensor_index = lax.axis_index("tp")
    turn = ctx_index.astype(jnp.int32).reshape(1)
    bias = bias_term.reshape(1, -1)

    query_recv = exchange(query_rows)

    pieces = []
    for shift in range(tensor):
        target = (tensor_index + shift) % tensor
        piece = lax.dynamic_slice_in_dim(grad_out, target * channels, channels, 1)
        if shift:
            piece = lax.ppermute(piece, "tp", [(i, (i + shift) % tensor) for i in range(tensor)])
        pieces.append(piece)
    grad_sources = (tensor_index - jnp.arange(tensor, dtype=jnp.int32)) % tensor

    both_packed = pack(turn, [key_rows, value_rows], shards)
    both_slots = permuted(both_packed)
    own = lax.dynamic_slice_in_dim(positions, ctx_index * slot_rows, slot_rows, 1)
    own_turned = jnp.concatenate(
        [lax.dynamic_slice_in_dim(own, ctx_index ^ number, 1, 0) for number in range(shards)], axis=1
    )

    filter_spec = filter_spectrum(filters, tables, both_packed[0])
    grad_seq, query_seq, grad_conv = settle_query(
        own.reshape(1, slots), query_recv, grad_sources, pieces, tokens, shards, [filter_spec]
    )
    grad_conv = gate(grad_conv, both_slots[1:])
    grad_recv = exchange(grad_conv)
    key_seq, value_seq, signal = settle_signal(
        turn, own_turned, both_slots, tokens, 1, grad_conv
    )
    signal_recv = [exchange(signal[0])]
    grad_signal, grad_spec = convolve(
        turn, [grad_recv], bias, filter_spec, tables, True, signal[0]
    )
    grad_signal_recv = exchange(grad_signal)
    conv_out, signal_spec = convolve(
        turn, signal_recv, bias, filter_spec, tables, False, grad_signal
    )
    conv_recv = exchange(conv_out)
    grad_filters = correlate(grad_spec, signal_spec, tables)
    grad_key, grad_value = final_products(
        grad_signal_recv, value_seq, key_seq, grad_filters, "key_value_gradients"
    )
    output, grad_query = final_products(
        conv_recv, query_seq, grad_seq, grad_key, "output_and_query_gradient"
    )
    return output, grad_query, grad_key, grad_value, grad_filters


def solution(mesh):
    return jax.shard_map(
        per_device,
        mesh=mesh,
        in_specs=(
            P("ctx", "tp"),
            P("ctx", "tp"),
            P("ctx", "tp"),
            P(),
            P(("tp", "ctx"), None),
            P(("tp", "ctx")),
            P(("ctx", "tp"), None),
        ),
        out_specs=(
            P("ctx", "tp"),
            P("ctx", "tp"),
            P("ctx", "tp"),
            P("ctx", "tp"),
            P(("tp", "ctx"), None),
        ),
        check_vma=False,
    )
```

```python
import functools
import math

import jax
import jax.numpy as jnp
import ml_dtypes
import numpy as np
from jax import lax
from jax.experimental import pallas as pl
from jax.experimental.pallas import tpu as pltpu
from jax.sharding import PartitionSpec as P

F32 = jnp.float32
BF16 = jnp.bfloat16
ROWS = 16
VMEM_LIMIT = 63_000_000


@functools.lru_cache(maxsize=None)
def dense_tables(shards, span):
    points = 2 * shards * span
    half = span // 2
    r = np.arange(span)
    forward = np.zeros((shards, 2 * span, 2 * span))
    for k1 in range(1, shards):
        bins = k1 + 2 * shards * np.arange(span)
        angle = (bins[:, None] * r[None, :] % points) * (2.0 * np.pi / points)
        cos, sin = np.cos(angle), np.sin(angle)
        forward[k1] = np.block([[cos, sin], [-sin, cos]])
    for place, k1 in ((0, 0), (1, shards)):
        bins = k1 + 2 * shards * np.arange(half)
        angle = (bins[:, None] * r[None, :] % points) * (2.0 * np.pi / points)
        columns = slice(place * span, place * span + span)
        forward[0, place * half : place * half + half, columns] = np.cos(angle)
        forward[0, span + place * half : span + place * half + half, columns] = -np.sin(angle)
    forward[0, span, :span] = 1.0 - 2.0 * (r % 2)
    inverse = 2.0 * np.transpose(forward, (0, 2, 1))
    inverse[0, :, 0] *= 0.5
    inverse[0, :, span] *= 0.5

    def parts(table):
        table = table.astype(np.float32)
        high = table.astype(ml_dtypes.bfloat16)
        low = (table - high.astype(np.float32)).astype(ml_dtypes.bfloat16)
        return high, low

    tops = [(parts(table)[0][:, :span], parts(table)[0][0, span:]) for table in (forward, inverse)]
    return parts(forward), tops


def plus(a, b):
    if a is None:
        return b
    return a if b is None else a + b


def minus(a, b):
    if b is None:
        return a
    return -b if a is None else a - b


def turned(z, step, count, sign):
    angle = sign * 2.0 * math.pi * (step % count) / count
    cos, sin = math.cos(angle), math.sin(angle)
    re, im = z
    if abs(sin) < 1e-9:
        return z if cos > 0 else (minus(None, re), minus(None, im))
    if abs(cos) < 1e-9:
        return (minus(None, im), re) if sin > 0 else (im, minus(None, re))
    if re is None and im is None:
        return z
    if im is None:
        return (re * cos, re * sin)
    if re is None:
        return (im * -sin, im * cos)
    if abs(abs(cos) - abs(sin)) < 1e-9:
        root = math.sqrt(0.5)
        first = re - im if sin * cos > 0 else re + im
        second = re + im if sin * cos > 0 else im - re
        c = root if cos > 0 else -root
        return (first * c, second * c)
    return (re * cos - im * sin, im * cos + re * sin)


def spread(values, sign):
    count = len(values)
    if count == 1:
        return values
    half = count // 2
    low, high = values[:half], values[half:]
    even = [(plus(a[0], b[0]), plus(a[1], b[1])) for a, b in zip(low, high)]
    odd = [
        turned((minus(a[0], b[0]), minus(a[1], b[1])), step, count, sign)
        for step, (a, b) in enumerate(zip(low, high))
    ]
    out = [None] * count
    out[0::2] = spread(even, sign)
    out[1::2] = spread(odd, sign)
    return out


def gather_up(values, sign):
    count = len(values)
    if count == 1:
        return values
    half = count // 2
    even = gather_up(values[0::2], sign)
    odd = [turned(z, step, count, sign) for step, z in enumerate(gather_up(values[1::2], sign))]
    return [(plus(a[0], b[0]), plus(a[1], b[1])) for a, b in zip(even, odd)] + [
        (minus(a[0], b[0]), minus(a[1], b[1])) for a, b in zip(even, odd)
    ]


def dot(a, b):
    return jnp.dot(a, b, preferred_element_type=F32)


def shard_transform(load, high_ref, low_ref=None):
    shards, rows, width = high_ref.shape
    span = rows // 2
    lanes = min(128, width)

    def body(step, carry):
        first = pl.multiple_of(step * ROWS, ROWS)
        for lane in range(0, width, lanes):
            values = [(load(i, pl.ds(first, ROWS), pl.ds(lane, lanes)), None) for i in range(shards)]
            values = spread(values + [(None, None)] * shards, -1)
            for k1 in range(shards):
                pair = (values[0][0], values[shards][0]) if k1 == 0 else values[k1]
                for part, value in enumerate(pair):
                    where = pl.ds(pl.multiple_of(part * span + first, ROWS), ROWS)
                    high = value.astype(BF16)
                    high_ref[k1, where, pl.ds(lane, lanes)] = high
                    if low_ref is not None:
                        low = (value - high.astype(F32)).astype(BF16)
                        low_ref[k1, where, pl.ds(lane, lanes)] = low
        return carry

    lax.fori_loop(0, span // ROWS, body, 0)


def shard_inverse(slab_ref, store):
    shards, rows, width = slab_ref.shape
    span = rows // 2
    lanes = min(128, width)

    def body(step, carry):
        first = pl.multiple_of(step * ROWS, ROWS)
        for lane in range(0, width, lanes):
            def load(k1, part):
                where = pl.ds(pl.multiple_of(part * span + first, ROWS), ROWS)
                return slab_ref[k1, where, pl.ds(lane, lanes)]

            values = [(load(0, 0), None)]
            values += [(load(k1, 0), load(k1, 1)) for k1 in range(1, shards)]
            values += [(load(0, 1), None)] + [(None, None)] * (shards - 1)
            values = gather_up(values, 1)
            for i in range(shards):
                store(i, pl.ds(first, ROWS), pl.ds(lane, lanes), values[i][0])
        return carry

    lax.fori_loop(0, span // ROWS, body, 0)


def bin_product(a, b, conjugate, first_slab):
    span = a.shape[0] // 2
    ar, ai, br, bi = a[:span], a[span:], b[:span], b[span:]
    cross = ai * bi
    shared = cross
    im = ai * br - ar * bi if conjugate else ar * bi + ai * br
    if first_slab is not False:
        alone = (lax.broadcasted_iota(jnp.int32, (span, 1), 0) == 0) & first_slab
        shared = jnp.where(alone, 0.0, cross)
        im = jnp.where(alone, cross, im)
    re = ar * br + shared if conjugate else ar * br - shared
    return jnp.concatenate([re.astype(BF16), im.astype(BF16)], axis=0)


def filter_kernel(filters_ref, fh_ref, fl_ref, after_ref, spec_ref, seq_ref, high_ref, low_ref):
    slab = pl.program_id(0)
    shards, span = seq_ref.shape[:2]

    @pl.when(slab == 0)
    def _():
        for i in range(shards):
            seq_ref[i] = filters_ref[:, i * span : (i + 1) * span].T
        shard_transform(lambda i, r, c: seq_ref[i, r, c], high_ref, low_ref)

    high = high_ref[slab]
    spec = dot(fh_ref[0], high) + dot(fh_ref[0], low_ref[slab]) + dot(fl_ref[0], high)
    spec_ref[0] = spec.astype(BF16)


class Table:
    def __init__(self, top_hbm, first_hbm, table_ref, sems):
        self.top, self.first, self.table, self.sems = top_hbm, first_hbm, table_ref, sems
        self.span = table_ref.shape[1] // 2

    def copies(self, slab):
        upper = pltpu.make_async_copy(
            self.top.at[slab], self.table.at[slab, pl.ds(0, self.span)], self.sems.at[slab]
        )
        if slab > 0:
            return [upper]
        lower = pltpu.make_async_copy(
            self.first, self.table.at[0, pl.ds(self.span, self.span)], self.sems.at[self.top.shape[0]]
        )
        return [upper, lower]

    def start(self, slab):
        for copy in self.copies(slab):
            copy.start()

    def ready(self, slab):
        for copy in self.copies(slab):
            copy.wait()
        span = self.span
        if slab > 0:
            self.table[slab, span:, :span] = -self.table[slab, :span, span:]
            self.table[slab, span:, span:] = self.table[slab, :span, :span]
        return self.table[slab]


def conv_kernel(conjugate, scale, n_in, n_out, turn_ref, *refs):
    pieces, refs = refs[:n_in], refs[n_in:]
    bias_ref, other_hbm, ft_hbm, f0_hbm, it_hbm, i0_hbm, after_ref = refs[:7]
    outs, refs = refs[7 : 7 + n_out], refs[7 + n_out :]
    spec_hbm, f_ref, i_ref, other_ref, spec_ref, high_ref, slab_ref = refs[:7]
    f_sems, i_sems, other_sems, out_sems, seq_ref, result_ref = refs[7:]
    shards = f_ref.shape[0]
    turn = turn_ref[0]
    forward_table = Table(ft_hbm, f0_hbm, f_ref, f_sems)
    inverse_table = Table(it_hbm, i0_hbm, i_ref, i_sems)

    def fetch(slab):
        return pltpu.make_async_copy(other_hbm.at[slab], other_ref.at[slab], other_sems.at[slab])

    def keep(slab):
        return pltpu.make_async_copy(spec_ref.at[slab], spec_hbm.at[slab], out_sems.at[slab])

    for slab in range(shards):
        forward_table.start(slab)
        fetch(slab).start()
        inverse_table.start(slab)
    if n_in > 1:
        for number in range(n_in):
            seq_ref[turn ^ number] = pieces[number][...]
    else:
        seq_ref = pieces[0]
    if n_out == 1:
        result_ref = outs[0]

    def load(i, rows, lanes):
        return seq_ref[i, rows, lanes].astype(F32)

    shard_transform(load, high_ref)

    def forward(slab):
        spec_ref[slab] = dot(forward_table.ready(slab), high_ref[slab])
        keep(slab).start()

    forward(0)
    for slab in range(shards):
        if slab + 1 < shards:
            forward(slab + 1)
        fetch(slab).wait()
        product = bin_product(spec_ref[slab], other_ref[slab].astype(F32), conjugate, slab == 0)
        slab_ref[slab] = dot(inverse_table.ready(slab), product)

    def store(i, rows, lanes, value):
        direct = bias_ref[:, lanes] * load(i, rows, lanes)
        result_ref[i, rows, lanes] = (direct + scale * value).astype(BF16)

    shard_inverse(slab_ref, store)
    if n_out > 1:
        for number in range(n_out):
            outs[number][...] = result_ref[turn ^ number]
    for slab in range(shards):
        keep(slab).wait()


def correlation_kernel(
    scale, a_hbm, b_hbm, it_hbm, i0_hbm, after_ref, out_ref, a_ref, b_ref, i_ref, slab_ref, seq_ref,
    i_sems, spec_sems,
):
    shards, span = seq_ref.shape[:2]
    inverse_table = Table(it_hbm, i0_hbm, i_ref, i_sems)

    def fetch(slab):
        return [
            pltpu.make_async_copy(source.at[slab], target.at[slab], spec_sems.at[which, slab])
            for which, (source, target) in enumerate(((a_hbm, a_ref), (b_hbm, b_ref)))
        ]

    for slab in range(shards):
        for copy in fetch(slab):
            copy.start()
        inverse_table.start(slab)
    for slab in range(shards):
        for copy in fetch(slab):
            copy.wait()
        product = bin_product(a_ref[slab], b_ref[slab], True, slab == 0)
        slab_ref[slab] = dot(inverse_table.ready(slab), product)

    def store(i, rows, lanes, value):
        seq_ref[i, rows, lanes] = scale * value

    shard_inverse(slab_ref, store)
    for i in range(shards):
        out_ref[:, i * span : (i + 1) * span] = seq_ref[i].T


def placement(own_ref, select_ref):
    tokens, slots = select_ref.shape
    token = lax.broadcasted_iota(jnp.int32, (tokens, slots), 0)
    select_ref[...] = jnp.where(token == own_ref[...], 1.0, 0.0).astype(BF16)


def pack_kernel(shards, turn_ref, *refs):
    sources, outs = refs[: -shards - 3], refs[-shards - 3 : -3]
    held, in_sems, out_sems = refs[-3:]
    rows = sources[0].shape[0] // shards

    def read(number, place):
        start = pl.multiple_of((turn_ref[0] ^ number) * rows, rows)
        return pltpu.make_async_copy(
            sources[place].at[pl.ds(start, rows)],
            held.at[number, pl.ds(place * rows, rows)],
            in_sems.at[number, place],
        )

    def write(number):
        return pltpu.make_async_copy(held.at[number], outs[number], out_sems.at[number])

    for number in range(shards):
        for place in range(len(sources)):
            read(number, place).start()
    for number in range(shards):
        for place in range(len(sources)):
            read(number, place).wait()
        write(number).start()
    for number in range(shards):
        write(number).wait()


def by_owner(turn, outs, value_ref):
    width = outs[0].shape[-1]
    parts = value_ref.shape[1] // width
    if len(outs) == 1:
        for part in range(parts):
            outs[0][part] = value_ref[:, part * width : (part + 1) * width]
        return
    for step in range(len(outs) // parts):

        @pl.when(pl.program_id(0) == step)
        def _(step=step):
            for part in range(parts):
                lanes = pl.ds(pl.multiple_of(((turn % parts) ^ part) * width, width), width)
                outs[step * parts + part][...] = value_ref[:, lanes]


def gate_kernel(*refs):
    pass


def settle_signal_kernel(shards, turn_ref, own_ref, after_ref, *refs):
    slots, (key_out, value_out), outs = refs[:shards], refs[shards : shards + 2], refs[shards + 2 : -2]
    select_ref, product_ref = refs[-2:]

    @pl.when(pl.program_id(0) == 0)
    def _():
        placement(own_ref, select_ref)

    slot_rows = slots[0].shape[0] // 2
    key = dot(select_ref[...], jnp.concatenate([slot[:slot_rows] for slot in slots], axis=0))
    value = dot(select_ref[...], jnp.concatenate([slot[slot_rows:] for slot in slots], axis=0))
    key_out[...] = key.astype(BF16)
    value_out[...] = value.astype(BF16)
    product_ref[...] = (key * value).astype(BF16)
    by_owner(turn_ref[0], outs, product_ref)


def settle_query_kernel(tensor, source_ref, own_ref, rows_ref, *refs):
    pieces = refs[:tensor]
    grad_out, query_out, out_ref, select_ref, product_ref = refs[-5:]

    @pl.when(pl.program_id(0) == 0)
    def _():
        placement(own_ref, select_ref)

    rows = pieces[0].shape[0]
    for number, piece in enumerate(pieces):
        start = pl.multiple_of(source_ref[number] * rows, rows)
        grad_out[pl.ds(start, rows), :] = piece[...]
    query = dot(select_ref[...], rows_ref[...])
    query_out[...] = query.astype(BF16)
    product_ref[...] = (query * grad_out[...].astype(F32)).astype(BF16)
    by_owner(None, [out_ref], product_ref)


def final_kernel(count, turn_ref, *refs):
    shared, (a_ref, b_ref, after_ref, a_out, b_out) = refs[:count], refs[count:]
    width = shared[0].shape[-1]
    parts = a_ref.shape[1] // width

    def products(factor, lanes):
        factor = factor.astype(F32)
        a_out[:, lanes] = (a_ref[:, lanes].astype(F32) * factor).astype(BF16)
        b_out[:, lanes] = (b_ref[:, lanes].astype(F32) * factor).astype(BF16)

    if count == 1:
        for part in range(parts):
            products(shared[0][part], slice(part * width, (part + 1) * width))
        return
    for step in range(count // parts):

        @pl.when(pl.program_id(0) == step)
        def _(step=step):
            for part in range(parts):
                start = pl.multiple_of(((turn_ref[0] % parts) ^ part) * width, width)
                products(shared[step * parts + part][...], pl.ds(start, width))


def cost(flops, moved):
    return pl.CostEstimate(flops=int(flops), bytes_accessed=int(moved), transcendentals=0)


def params():
    return pltpu.CompilerParams(
        dimension_semantics=("arbitrary",), vmem_limit_bytes=VMEM_LIMIT
    )


def whole(shape):
    return pl.BlockSpec(shape, lambda j, *turn: (0,) * len(shape))


def slab_of(shape):
    return pl.BlockSpec((1,) + shape[1:], lambda j, *turn: (j, 0, 0))


UNREAD = pl.BlockSpec(memory_space=pl.ANY)


def shape_of(shape, dtype):
    return jax.ShapeDtypeStruct(shape, dtype)


def filter_spectrum(filters, tables, after):
    fh, fl = tables[0]
    width, length = filters.shape
    shards, rows, _ = fh.shape
    spec = (shards, rows, width)
    return pl.pallas_call(
        filter_kernel,
        grid=(shards,),
        in_specs=[whole(filters.shape), slab_of(fh.shape), slab_of(fl.shape), UNREAD],
        out_specs=slab_of(spec),
        out_shape=shape_of(spec, BF16),
        scratch_shapes=[
            pltpu.VMEM((shards, rows // 2, width), F32),
            pltpu.VMEM(spec, BF16),
            pltpu.VMEM(spec, BF16),
        ],
        compiler_params=params(),
        cost_estimate=cost(1e12, 1e9),
        name="filter_spectrum",
    )(filters, fh, fl, after)


def convolve(turn, pieces, bias, other, tables, conjugate, n_out, after):
    (ft, f0), (it, i0) = tables[1]
    shards, rows, width = other.shape
    tokens = rows // 2
    spec = (shards, rows, width)
    seq = (shards, tokens, width)
    out = seq if n_out == 1 else seq[1:]
    length = shards * tokens
    scale = 1.0 / (2 * length * math.sqrt(length))
    outs = pl.pallas_call(
        functools.partial(conv_kernel, conjugate, scale, len(pieces), n_out),
        grid_spec=pltpu.PrefetchScalarGridSpec(
            num_scalar_prefetch=1,
            grid=(1,),
            in_specs=[whole(piece.shape) for piece in pieces] + [whole(bias.shape)] + [UNREAD] * 6,
            out_specs=[whole(out)] * n_out + [UNREAD],
            scratch_shapes=[
                pltpu.VMEM((shards, rows, rows), BF16),
                pltpu.VMEM((shards, rows, rows), BF16),
                pltpu.VMEM(spec, BF16),
                pltpu.VMEM(spec, F32),
                pltpu.VMEM(spec, BF16),
                pltpu.VMEM(spec, F32),
                pltpu.SemaphoreType.DMA((shards + 1,)),
                pltpu.SemaphoreType.DMA((shards + 1,)),
                pltpu.SemaphoreType.DMA((shards,)),
                pltpu.SemaphoreType.DMA((shards,)),
                pltpu.VMEM(seq, BF16),
                pltpu.VMEM(seq, BF16),
            ],
        ),
        out_shape=[shape_of(out, BF16)] * n_out + [shape_of(spec, F32)],
        compiler_params=params(),
        cost_estimate=cost(4 * shards * rows * rows * width, 4 * ft.size + 10 * shards * rows * width),
        name="convolve_backward" if conjugate else "convolve_forward",
    )(turn, *pieces, bias, other, ft, f0, it, i0, after)
    return outs[:-1], outs[-1]


def correlate(spec_a, spec_b, tables, after):
    it, i0 = tables[1][1]
    shards, rows, width = spec_a.shape
    length = shards * rows // 2
    scale = 1.0 / (2 * length * math.sqrt(length))
    return pl.pallas_call(
        functools.partial(correlation_kernel, scale),
        grid=(1,),
        in_specs=[UNREAD] * 5,
        out_specs=whole((width, length)),
        out_shape=shape_of((width, length), F32),
        scratch_shapes=[
            pltpu.VMEM(spec_a.shape, F32),
            pltpu.VMEM(spec_a.shape, F32),
            pltpu.VMEM((shards, rows, rows), BF16),
            pltpu.VMEM(spec_a.shape, F32),
            pltpu.VMEM((shards, rows // 2, width), F32),
            pltpu.SemaphoreType.DMA((shards + 1,)),
            pltpu.SemaphoreType.DMA((2, shards)),
        ],
        compiler_params=params(),
        cost_estimate=cost(2 * shards * rows * rows * width, 2 * it.size + 12 * spec_a.size),
        name="filter_gradient",
    )(spec_a, spec_b, it, i0, after)


def pack(turn, arrays, shards):
    rows, channels = arrays[0].shape
    rows = len(arrays) * rows // shards
    moved = 4 * len(arrays) * arrays[0].size
    return pl.pallas_call(
        functools.partial(pack_kernel, shards),
        grid_spec=pltpu.PrefetchScalarGridSpec(
            num_scalar_prefetch=1,
            grid=(1,),
            in_specs=[pl.BlockSpec(memory_space=pl.ANY)] * len(arrays),
            out_specs=[pl.BlockSpec(memory_space=pl.ANY)] * shards,
            scratch_shapes=[
                pltpu.VMEM((shards, rows, channels), arrays[0].dtype),
                pltpu.SemaphoreType.DMA((shards, len(arrays))),
                pltpu.SemaphoreType.DMA((shards,)),
            ],
        ),
        out_shape=[shape_of((rows, channels), arrays[0].dtype)] * shards,
        compiler_params=params(),
        cost_estimate=cost(0, moved),
        name="pack_rows",
    )(turn, *arrays)


def column_plan(channels, shards, lanes):
    width = channels // shards
    parts = min(shards, max(1, lanes // width))
    return width, parts, parts * width, shards // parts


def column(rows, block):
    return pl.BlockSpec((rows, block), lambda j: (0, j))


def turned_column(rows, block, parts, pieces):
    if pieces:
        return pl.BlockSpec((rows, block), lambda j, turn: (0, j ^ (turn[0] // parts)))
    return pl.BlockSpec((rows, block), lambda j, turn: (0, j))


def gate(value, after):
    return pl.pallas_call(
        gate_kernel,
        in_specs=[UNREAD] * (1 + len(after)),
        out_specs=UNREAD,
        out_shape=shape_of(value.shape, value.dtype),
        input_output_aliases={0: 0},
        name="gate",
    )(value, *after)


def settle_signal(turn, own, slots, tokens, n_out, after):
    shards = len(slots)
    slot_rows, channels = slots[0].shape
    count = shards * slot_rows // 2
    width, parts, block, steps = column_plan(channels, shards, 512)
    seq = shape_of((tokens, channels), BF16)
    column_at = functools.partial(turned_column, block=block, parts=parts, pieces=n_out > 1)
    if n_out > 1:
        out_spec, out_shape = whole((tokens, width)), shape_of((tokens, width), BF16)
    else:
        out_spec = pl.BlockSpec((parts, tokens, width), lambda j, turn: (j, 0, 0))
        out_shape = shape_of((shards, tokens, width), BF16)
    outs = pl.pallas_call(
        functools.partial(settle_signal_kernel, shards),
        grid_spec=pltpu.PrefetchScalarGridSpec(
            num_scalar_prefetch=1,
            grid=(steps,),
            in_specs=[whole(own.shape), UNREAD] + [column_at(slot_rows)] * shards,
            out_specs=[column_at(tokens)] * 2 + [out_spec] * n_out,
            scratch_shapes=[pltpu.VMEM((tokens, count), BF16), pltpu.VMEM((tokens, block), BF16)],
        ),
        out_shape=[seq, seq] + [out_shape] * n_out,
        compiler_params=params(),
        cost_estimate=cost(4 * tokens * count * channels, 4 * count * channels + 6 * tokens * channels),
        name="settle_signal",
    )(turn, own, after, *slots)
    return outs[0], outs[1], outs[2:]


def settle_query(own, rows, sources, pieces, tokens, shards, after):
    count, channels = rows.shape
    width, parts, block, steps = column_plan(channels, shards, 512)
    seq = shape_of((tokens, channels), BF16)
    return pl.pallas_call(
        functools.partial(settle_query_kernel, len(pieces)),
        grid=(steps,),
        in_specs=[pl.BlockSpec(memory_space=pltpu.SMEM), whole(own.shape), column(count, block)]
        + [column(piece.shape[0], block) for piece in pieces]
        + [UNREAD] * len(after),
        out_specs=[column(tokens, block)] * 2
        + [pl.BlockSpec((parts, tokens, width), lambda j: (j, 0, 0))],
        out_shape=[seq, seq, shape_of((shards, tokens, width), BF16)],
        scratch_shapes=[pltpu.VMEM((tokens, count), BF16), pltpu.VMEM((tokens, block), BF16)],
        compiler_params=params(),
        cost_estimate=cost(2 * tokens * count * channels, 2 * count * channels + 8 * tokens * channels),
        name="settle_query",
    )(sources, own, rows, *pieces, *after)


def final_products(turn, shared, a, b, shards, after, name):
    tokens, width = shared[0].shape[-2:]
    _, parts, block, steps = column_plan(a.shape[1], shards, 1024)
    pieces = len(shared) > 1
    column_at = turned_column(tokens, block, parts, pieces)
    if pieces:
        shared_spec = whole((tokens, width))
    else:
        shared_spec = pl.BlockSpec((parts, tokens, width), lambda j, turn: (j, 0, 0))
    return pl.pallas_call(
        functools.partial(final_kernel, len(shared)),
        grid_spec=pltpu.PrefetchScalarGridSpec(
            num_scalar_prefetch=1,
            grid=(steps,),
            in_specs=[shared_spec] * len(shared) + [column_at, column_at, UNREAD],
            out_specs=[column_at, column_at],
        ),
        out_shape=[shape_of(a.shape, BF16)] * 2,
        compiler_params=params(),
        cost_estimate=cost(2 * a.size, 10 * a.size),
        name=name,
    )(turn, *shared, a, b, after)


def permuted(pieces):
    shards = len(pieces)
    order = sorted(range(1, shards), key=lambda number: (number < 2, number & 1, number))
    received = {
        number: lax.ppermute(pieces[number], "ctx", [(i, i ^ number) for i in range(shards)])
        for number in order
    }
    return [pieces[0]] + [received[number] for number in range(1, shards)]


def exchange(value):
    return lax.all_to_all(value, "ctx", split_axis=0, concat_axis=0, tiled=True)


def per_device(query_rows, key_rows, value_rows, positions, filters, bias_term, grad_out):
    shards = lax.axis_size("ctx")
    ctx_index = lax.axis_index("ctx")
    slots, channels = query_rows.shape
    slot_rows = slots // shards
    tokens = filters.shape[1] // shards
    tables = dense_tables(shards, tokens)

    tensor = lax.axis_size("tp")
    tensor_index = lax.axis_index("tp")
    turn = ctx_index.astype(jnp.int32).reshape(1)
    bias = bias_term.reshape(1, -1)

    query_recv = exchange(query_rows)

    pieces = []
    for shift in range(tensor):
        target = (tensor_index + shift) % tensor
        piece = lax.dynamic_slice_in_dim(grad_out, target * channels, channels, 1)
        if shift:
            piece = lax.ppermute(piece, "tp", [(i, (i + shift) % tensor) for i in range(tensor)])
        pieces.append(piece)
    grad_sources = (tensor_index - jnp.arange(tensor, dtype=jnp.int32)) % tensor

    both_packed = pack(turn, [key_rows, value_rows], shards)
    both_slots = permuted(both_packed)
    own = lax.dynamic_slice_in_dim(positions, ctx_index * slot_rows, slot_rows, 1)
    own_turned = jnp.concatenate(
        [lax.dynamic_slice_in_dim(own, ctx_index ^ number, 1, 0) for number in range(shards)], axis=1
    )

    grad_seq, query_seq, grad_conv = settle_query(
        own.reshape(1, slots), query_recv, grad_sources, pieces, tokens, shards, [both_packed[0]]
    )
    grad_recv = exchange(grad_conv)
    filter_spec = filter_spectrum(filters, tables, grad_conv)
    (grad_signal,), grad_spec = convolve(
        turn, [grad_recv], bias, filter_spec, tables, True, 1, filter_spec
    )
    n_pieces = shards if (channels // shards) % 128 == 0 else 1
    key_seq, value_seq, signal = settle_signal(
        turn, own_turned, both_slots, tokens, n_pieces, grad_signal
    )
    signal_recv = permuted(signal) if n_pieces > 1 else [exchange(signal[0])]
    grad_signal = gate(grad_signal, signal_recv)
    grad_signal_recv = exchange(grad_signal)
    conv_out, signal_spec = convolve(
        turn, signal_recv, bias, filter_spec, tables, False, n_pieces, grad_signal
    )
    conv_recv = permuted(conv_out) if n_pieces > 1 else [exchange(conv_out[0])]
    grad_filters = correlate(grad_spec, signal_spec, tables, grad_signal_recv)
    grad_key, grad_value = final_products(
        turn, [grad_signal_recv], value_seq, key_seq, shards, grad_filters, "key_value_gradients"
    )
    output, grad_query = final_products(
        turn, conv_recv, query_seq, grad_seq, shards, grad_key, "output_and_query_gradient"
    )
    return output, grad_query, grad_key, grad_value, grad_filters


def solution(mesh):
    return jax.shard_map(
        per_device,
        mesh=mesh,
        in_specs=(
            P("ctx", "tp"),
            P("ctx", "tp"),
            P("ctx", "tp"),
            P(),
            P(("tp", "ctx"), None),
            P(("tp", "ctx")),
            P(("ctx", "tp"), None),
        ),
        out_specs=(
            P("ctx", "tp"),
            P("ctx", "tp"),
            P("ctx", "tp"),
            P("ctx", "tp"),
            P(("tp", "ctx"), None),
        ),
        check_vma=False,
    )
```

```python
import functools
import math

import jax
import jax.numpy as jnp
import ml_dtypes
import numpy as np
from jax import lax
from jax.experimental import pallas as pl
from jax.experimental.pallas import tpu as pltpu
from jax.sharding import PartitionSpec as P

F32 = jnp.float32
BF16 = jnp.bfloat16
ROWS = 16
VMEM_LIMIT = 63_000_000


@functools.lru_cache(maxsize=None)
def dense_tables(shards, span):
    points = 2 * shards * span
    half = span // 2
    r = np.arange(span)
    forward = np.zeros((shards, 2 * span, 2 * span))
    for k1 in range(1, shards):
        bins = k1 + 2 * shards * np.arange(span)
        angle = (bins[:, None] * r[None, :] % points) * (2.0 * np.pi / points)
        cos, sin = np.cos(angle), np.sin(angle)
        forward[k1] = np.block([[cos, sin], [-sin, cos]])
    for place, k1 in ((0, 0), (1, shards)):
        bins = k1 + 2 * shards * np.arange(half)
        angle = (bins[:, None] * r[None, :] % points) * (2.0 * np.pi / points)
        columns = slice(place * span, place * span + span)
        forward[0, place * half : place * half + half, columns] = np.cos(angle)
        forward[0, span + place * half : span + place * half + half, columns] = -np.sin(angle)
    forward[0, span, :span] = 1.0 - 2.0 * (r % 2)
    inverse = 2.0 * np.transpose(forward, (0, 2, 1))
    inverse[0, :, 0] *= 0.5
    inverse[0, :, span] *= 0.5

    def parts(table):
        table = table.astype(np.float32)
        high = table.astype(ml_dtypes.bfloat16)
        low = (table - high.astype(np.float32)).astype(ml_dtypes.bfloat16)
        return high, low

    return parts(forward), parts(inverse)


def plus(a, b):
    if a is None:
        return b
    return a if b is None else a + b


def minus(a, b):
    if b is None:
        return a
    return -b if a is None else a - b


def turned(z, step, count, sign):
    angle = sign * 2.0 * math.pi * (step % count) / count
    cos, sin = math.cos(angle), math.sin(angle)
    re, im = z
    if abs(sin) < 1e-9:
        return z if cos > 0 else (minus(None, re), minus(None, im))
    if abs(cos) < 1e-9:
        return (minus(None, im), re) if sin > 0 else (im, minus(None, re))
    if re is None and im is None:
        return z
    if im is None:
        return (re * cos, re * sin)
    if re is None:
        return (im * -sin, im * cos)
    if abs(abs(cos) - abs(sin)) < 1e-9:
        root = math.sqrt(0.5)
        first = re - im if sin * cos > 0 else re + im
        second = re + im if sin * cos > 0 else im - re
        c = root if cos > 0 else -root
        return (first * c, second * c)
    return (re * cos - im * sin, im * cos + re * sin)


def spread(values, sign):
    count = len(values)
    if count == 1:
        return values
    half = count // 2
    low, high = values[:half], values[half:]
    even = [(plus(a[0], b[0]), plus(a[1], b[1])) for a, b in zip(low, high)]
    odd = [
        turned((minus(a[0], b[0]), minus(a[1], b[1])), step, count, sign)
        for step, (a, b) in enumerate(zip(low, high))
    ]
    out = [None] * count
    out[0::2] = spread(even, sign)
    out[1::2] = spread(odd, sign)
    return out


def gather_up(values, sign):
    count = len(values)
    if count == 1:
        return values
    half = count // 2
    even = gather_up(values[0::2], sign)
    odd = [turned(z, step, count, sign) for step, z in enumerate(gather_up(values[1::2], sign))]
    return [(plus(a[0], b[0]), plus(a[1], b[1])) for a, b in zip(even, odd)] + [
        (minus(a[0], b[0]), minus(a[1], b[1])) for a, b in zip(even, odd)
    ]


def dot(a, b):
    return jnp.dot(a, b, preferred_element_type=F32)


def shard_transform(load, high_ref, low_ref=None):
    shards, rows, width = high_ref.shape
    span = rows // 2
    lanes = min(128, width)

    def body(step, carry):
        first = pl.multiple_of(step * ROWS, ROWS)
        for lane in range(0, width, lanes):
            values = [(load(i, pl.ds(first, ROWS), pl.ds(lane, lanes)), None) for i in range(shards)]
            values = spread(values + [(None, None)] * shards, -1)
            for k1 in range(shards):
                pair = (values[0][0], values[shards][0]) if k1 == 0 else values[k1]
                for part, value in enumerate(pair):
                    where = pl.ds(pl.multiple_of(part * span + first, ROWS), ROWS)
                    high = value.astype(BF16)
                    high_ref[k1, where, pl.ds(lane, lanes)] = high
                    if low_ref is not None:
                        low = (value - high.astype(F32)).astype(BF16)
                        low_ref[k1, where, pl.ds(lane, lanes)] = low
        return carry

    lax.fori_loop(0, span // ROWS, body, 0)


def shard_inverse(slab_ref, store):
    shards, rows, width = slab_ref.shape
    span = rows // 2
    lanes = min(128, width)

    def body(step, carry):
        first = pl.multiple_of(step * ROWS, ROWS)
        for lane in range(0, width, lanes):
            def load(k1, part):
                where = pl.ds(pl.multiple_of(part * span + first, ROWS), ROWS)
                return slab_ref[k1, where, pl.ds(lane, lanes)]

            values = [(load(0, 0), None)]
            values += [(load(k1, 0), load(k1, 1)) for k1 in range(1, shards)]
            values += [(load(0, 1), None)] + [(None, None)] * (shards - 1)
            values = gather_up(values, 1)
            for i in range(shards):
                store(i, pl.ds(first, ROWS), pl.ds(lane, lanes), values[i][0])
        return carry

    lax.fori_loop(0, span // ROWS, body, 0)


def bin_product(a, b, conjugate, first_slab):
    span = a.shape[0] // 2
    ar, ai, br, bi = a[:span], a[span:], b[:span], b[span:]
    cross = ai * bi
    shared = cross
    im = ai * br - ar * bi if conjugate else ar * bi + ai * br
    if first_slab is not False:
        alone = (lax.broadcasted_iota(jnp.int32, (span, 1), 0) == 0) & first_slab
        shared = jnp.where(alone, 0.0, cross)
        im = jnp.where(alone, cross, im)
    re = ar * br + shared if conjugate else ar * br - shared
    return jnp.concatenate([re.astype(BF16), im.astype(BF16)], axis=0)


def filter_kernel(filters_ref, fh_ref, fl_ref, after_ref, spec_ref, seq_ref, high_ref, low_ref):
    slab = pl.program_id(0)
    shards, span = seq_ref.shape[:2]

    @pl.when(slab == 0)
    def _():
        for i in range(shards):
            seq_ref[i] = filters_ref[:, i * span : (i + 1) * span].T
        shard_transform(lambda i, r, c: seq_ref[i, r, c], high_ref, low_ref)

    high = high_ref[slab]
    spec_ref[0] = dot(fh_ref[0], high) + dot(fh_ref[0], low_ref[slab]) + dot(fl_ref[0], high)


def conv_kernel(conjugate, scale, n_in, turn_ref, *refs):
    pieces, refs = refs[:n_in], refs[n_in:]
    bias_ref, other_hbm, fh_hbm, ih_hbm, after_ref, out_ref, spec_hbm = refs[:7]
    fh_ref, ih_ref, other_ref, spec_ref, high_ref, slab_ref, in_sems, out_sems = refs[7:15]
    seq_ref = pieces[0] if n_in == 1 else refs[15]
    shards = fh_ref.shape[0]

    def fetch(which, slab):
        source, target = ((fh_hbm, fh_ref), (other_hbm, other_ref), (ih_hbm, ih_ref))[which]
        return pltpu.make_async_copy(source.at[slab], target.at[slab], in_sems.at[which, slab])

    def keep(slab):
        return pltpu.make_async_copy(spec_ref.at[slab], spec_hbm.at[slab], out_sems.at[slab])

    for slab in range(shards):
        for which in range(3):
            fetch(which, slab).start()
    if n_in > 1:
        for number in range(n_in):
            seq_ref[turn_ref[0] ^ number] = pieces[number][...]

    def load(i, rows, lanes):
        return seq_ref[i, rows, lanes].astype(F32)

    shard_transform(load, high_ref)

    def forward(slab):
        fetch(0, slab).wait()
        spec_ref[slab] = dot(fh_ref[slab], high_ref[slab])
        keep(slab).start()

    forward(0)
    for slab in range(shards):
        if slab + 1 < shards:
            forward(slab + 1)
        fetch(1, slab).wait()
        product = bin_product(spec_ref[slab], other_ref[slab], conjugate, slab == 0)
        fetch(2, slab).wait()
        slab_ref[slab] = dot(ih_ref[slab], product)

    def store(i, rows, lanes, value):
        direct = bias_ref[:, lanes] * load(i, rows, lanes)
        out_ref[i, rows, lanes] = (direct + scale * value).astype(BF16)

    shard_inverse(slab_ref, store)
    for slab in range(shards):
        keep(slab).wait()


def correlation_kernel(scale, spec_ref, other_ref, ih_ref, out_ref, slab_ref, seq_ref):
    slab = pl.program_id(0)
    shards = pl.num_programs(0)
    span = seq_ref.shape[1]
    slab_ref[slab] = dot(ih_ref[0], bin_product(spec_ref[0], other_ref[0], True, slab == 0))

    @pl.when(slab == shards - 1)
    def _():
        def store(i, rows, lanes, value):
            seq_ref[i, rows, lanes] = scale * value

        shard_inverse(slab_ref, store)
        for i in range(seq_ref.shape[0]):
            out_ref[:, i * span : (i + 1) * span] = seq_ref[i].T


def placement(own_ref, select_ref):
    tokens, slots = select_ref.shape
    token = lax.broadcasted_iota(jnp.int32, (tokens, slots), 0)
    select_ref[...] = jnp.where(token == own_ref[...], 1.0, 0.0).astype(BF16)


def travel_order(shards):
    return [0] + sorted(range(1, shards), key=lambda number: (number < 2, number & 1, number))


def pack_kernel(shards, turn_ref, *refs):
    sources, outs = refs[: -shards - 3], refs[-shards - 3 : -3]
    held, in_sems, out_sems = refs[-3:]
    rows = sources[0].shape[0] // shards

    def read(number, place):
        start = pl.multiple_of((turn_ref[0] ^ travel_order(shards)[number]) * rows, rows)
        return pltpu.make_async_copy(
            sources[place].at[pl.ds(start, rows)],
            held.at[number, pl.ds(place * rows, rows)],
            in_sems.at[number, place],
        )

    def write(number):
        return pltpu.make_async_copy(held.at[number], outs[number], out_sems.at[number])

    for number in range(shards):
        for place in range(len(sources)):
            read(number, place).start()
    for number in range(shards):
        for place in range(len(sources)):
            read(number, place).wait()
        write(number).start()
    for number in range(shards):
        write(number).wait()


def by_owner(turn, outs, value_ref):
    width = outs[0].shape[-1]
    parts = value_ref.shape[1] // width
    if len(outs) == 1:
        for part in range(parts):
            outs[0][part] = value_ref[:, part * width : (part + 1) * width]
        return
    for step in range(len(outs) // parts):

        @pl.when(pl.program_id(0) == step)
        def _(step=step):
            for part in range(parts):
                lanes = pl.ds(pl.multiple_of(((turn % parts) ^ part) * width, width), width)
                outs[step * parts + part][...] = value_ref[:, lanes]


def gate_kernel(*refs):
    pass


def settle_signal_kernel(shards, turn_ref, own_ref, after_ref, *refs):
    slots, (key_out, value_out), outs = refs[:shards], refs[shards : shards + 2], refs[shards + 2 : -2]
    select_ref, product_ref = refs[-2:]

    @pl.when(pl.program_id(0) == 0)
    def _():
        placement(own_ref, select_ref)

    slot_rows = slots[0].shape[0] // 2
    key = dot(select_ref[...], jnp.concatenate([slot[:slot_rows] for slot in slots], axis=0))
    value = dot(select_ref[...], jnp.concatenate([slot[slot_rows:] for slot in slots], axis=0))
    key_out[...] = key.astype(BF16)
    value_out[...] = value.astype(BF16)
    product_ref[...] = (key * value).astype(BF16)
    by_owner(turn_ref[0], outs, product_ref)


def settle_query_kernel(tensor, source_ref, own_ref, rows_ref, *refs):
    pieces = refs[:tensor]
    grad_out, query_out, out_ref, select_ref, product_ref = refs[-5:]

    @pl.when(pl.program_id(0) == 0)
    def _():
        placement(own_ref, select_ref)

    rows = pieces[0].shape[0]
    for number, piece in enumerate(pieces):
        start = pl.multiple_of(source_ref[number] * rows, rows)
        grad_out[pl.ds(start, rows), :] = piece[...]
    query = dot(select_ref[...], rows_ref[...])
    query_out[...] = query.astype(BF16)
    product_ref[...] = (query * grad_out[...].astype(F32)).astype(BF16)
    by_owner(None, [out_ref], product_ref)


def final_kernel(shared_ref, a_ref, b_ref, after_ref, a_out, b_out):
    width = shared_ref.shape[2]
    for part in range(shared_ref.shape[0]):
        lanes = slice(part * width, (part + 1) * width)
        shared = shared_ref[part].astype(F32)
        a_out[:, lanes] = (a_ref[:, lanes].astype(F32) * shared).astype(BF16)
        b_out[:, lanes] = (b_ref[:, lanes].astype(F32) * shared).astype(BF16)


def cost(flops, moved):
    return pl.CostEstimate(flops=int(flops), bytes_accessed=int(moved), transcendentals=0)


def params():
    return pltpu.CompilerParams(
        dimension_semantics=("arbitrary",), vmem_limit_bytes=VMEM_LIMIT
    )


def whole(shape):
    return pl.BlockSpec(shape, lambda j, *turn: (0,) * len(shape))


def slab_of(shape):
    return pl.BlockSpec((1,) + shape[1:], lambda j, *turn: (j, 0, 0))


UNREAD = pl.BlockSpec(memory_space=pl.ANY)


def shape_of(shape, dtype):
    return jax.ShapeDtypeStruct(shape, dtype)


def filter_spectrum(filters, tables, after):
    (fh, fl), _ = tables
    width, length = filters.shape
    shards, rows, _ = fh.shape
    spec = (shards, rows, width)
    return pl.pallas_call(
        filter_kernel,
        grid=(shards,),
        in_specs=[whole(filters.shape), slab_of(fh.shape), slab_of(fl.shape), UNREAD],
        out_specs=slab_of(spec),
        out_shape=shape_of(spec, F32),
        scratch_shapes=[
            pltpu.VMEM((shards, rows // 2, width), F32),
            pltpu.VMEM(spec, BF16),
            pltpu.VMEM(spec, BF16),
        ],
        compiler_params=params(),
        cost_estimate=cost(1e12, 1e9),
        name="filter_spectrum",
    )(filters, fh, fl, after)


def convolve(turn, pieces, bias, other, tables, conjugate, after):
    (fh, _), (ih, _) = tables
    shards, rows, _ = fh.shape
    tokens, width = pieces[0].shape[-2:]
    spec = (shards, rows, width)
    seq = (shards, tokens, width)
    length = shards * tokens
    scale = 1.0 / (2 * length * math.sqrt(length))
    return pl.pallas_call(
        functools.partial(conv_kernel, conjugate, scale, len(pieces)),
        grid_spec=pltpu.PrefetchScalarGridSpec(
            num_scalar_prefetch=1,
            grid=(1,),
            in_specs=[whole(piece.shape) for piece in pieces] + [whole(bias.shape)] + [UNREAD] * 4,
            out_specs=[whole(seq), UNREAD],
            scratch_shapes=[
                pltpu.VMEM(fh.shape, BF16),
                pltpu.VMEM(ih.shape, BF16),
                pltpu.VMEM(spec, F32),
                pltpu.VMEM(spec, F32),
                pltpu.VMEM(spec, BF16),
                pltpu.VMEM(spec, F32),
                pltpu.SemaphoreType.DMA((3, shards)),
                pltpu.SemaphoreType.DMA((shards,)),
            ]
            + [pltpu.VMEM(seq, BF16)] * (len(pieces) > 1),
        ),
        out_shape=[shape_of(seq, BF16), shape_of(spec, F32)],
        compiler_params=params(),
        cost_estimate=cost(4 * shards * rows * rows * width, 4 * fh.size + 12 * shards * rows * width),
        name="convolve_backward" if conjugate else "convolve_forward",
    )(turn, *pieces, bias, other, fh, ih, after)


def correlate(spec_a, spec_b, tables):
    _, (ih, _) = tables
    shards, rows, width = spec_a.shape
    length = shards * rows // 2
    scale = 1.0 / (2 * length * math.sqrt(length))
    return pl.pallas_call(
        functools.partial(correlation_kernel, scale),
        grid=(shards,),
        in_specs=[slab_of(spec_a.shape), slab_of(spec_b.shape), slab_of(ih.shape)],
        out_specs=whole((width, length)),
        out_shape=shape_of((width, length), F32),
        scratch_shapes=[
            pltpu.VMEM(spec_a.shape, F32),
            pltpu.VMEM((shards, rows // 2, width), F32),
        ],
        compiler_params=params(),
        cost_estimate=cost(4 * shards * rows * rows * width, 2 * ih.size + 12 * spec_a.size),
        name="filter_gradient",
    )(spec_a, spec_b, ih)


def pack(turn, arrays, shards):
    rows, channels = arrays[0].shape
    rows = len(arrays) * rows // shards
    moved = 4 * len(arrays) * arrays[0].size
    return pl.pallas_call(
        functools.partial(pack_kernel, shards),
        grid_spec=pltpu.PrefetchScalarGridSpec(
            num_scalar_prefetch=1,
            grid=(1,),
            in_specs=[pl.BlockSpec(memory_space=pl.ANY)] * len(arrays),
            out_specs=[pl.BlockSpec(memory_space=pl.ANY)] * shards,
            scratch_shapes=[
                pltpu.VMEM((shards, rows, channels), arrays[0].dtype),
                pltpu.SemaphoreType.DMA((shards, len(arrays))),
                pltpu.SemaphoreType.DMA((shards,)),
            ],
        ),
        out_shape=[shape_of((rows, channels), arrays[0].dtype)] * shards,
        compiler_params=params(),
        cost_estimate=cost(0, moved),
        name="pack_rows",
    )(turn, *arrays)


def column_plan(channels, shards, lanes):
    width = channels // shards
    parts = min(shards, max(1, lanes // width))
    return width, parts, parts * width, shards // parts


def column(rows, block):
    return pl.BlockSpec((rows, block), lambda j: (0, j))


def turned_column(rows, block, parts, pieces):
    if pieces:
        return pl.BlockSpec((rows, block), lambda j, turn: (0, j ^ (turn[0] // parts)))
    return pl.BlockSpec((rows, block), lambda j, turn: (0, j))


def gate(value, after):
    return pl.pallas_call(
        gate_kernel,
        in_specs=[UNREAD] * (1 + len(after)),
        out_specs=UNREAD,
        out_shape=shape_of(value.shape, value.dtype),
        input_output_aliases={0: 0},
        name="gate",
    )(value, *after)


def settle_signal(turn, own, slots, tokens, n_out, after):
    shards = len(slots)
    slot_rows, channels = slots[0].shape
    count = shards * slot_rows // 2
    width, parts, block, steps = column_plan(channels, shards, 512)
    seq = shape_of((tokens, channels), BF16)
    column_at = functools.partial(turned_column, block=block, parts=parts, pieces=n_out > 1)
    if n_out > 1:
        out_spec, out_shape = whole((tokens, width)), shape_of((tokens, width), BF16)
    else:
        out_spec = pl.BlockSpec((parts, tokens, width), lambda j, turn: (j, 0, 0))
        out_shape = shape_of((shards, tokens, width), BF16)
    outs = pl.pallas_call(
        functools.partial(settle_signal_kernel, shards),
        grid_spec=pltpu.PrefetchScalarGridSpec(
            num_scalar_prefetch=1,
            grid=(steps,),
            in_specs=[whole(own.shape), UNREAD] + [column_at(slot_rows)] * shards,
            out_specs=[column_at(tokens)] * 2 + [out_spec] * n_out,
            scratch_shapes=[pltpu.VMEM((tokens, count), BF16), pltpu.VMEM((tokens, block), BF16)],
        ),
        out_shape=[seq, seq] + [out_shape] * n_out,
        compiler_params=params(),
        cost_estimate=cost(4 * tokens * count * channels, 4 * count * channels + 6 * tokens * channels),
        name="settle_signal",
    )(turn, own, after, *slots)
    return outs[0], outs[1], outs[2:]


def settle_query(own, rows, sources, pieces, tokens, shards, after):
    count, channels = rows.shape
    width, parts, block, steps = column_plan(channels, shards, 512)
    seq = shape_of((tokens, channels), BF16)
    return pl.pallas_call(
        functools.partial(settle_query_kernel, len(pieces)),
        grid=(steps,),
        in_specs=[pl.BlockSpec(memory_space=pltpu.SMEM), whole(own.shape), column(count, block)]
        + [column(piece.shape[0], block) for piece in pieces]
        + [UNREAD] * len(after),
        out_specs=[column(tokens, block)] * 2
        + [pl.BlockSpec((parts, tokens, width), lambda j: (j, 0, 0))],
        out_shape=[seq, seq, shape_of((shards, tokens, width), BF16)],
        scratch_shapes=[pltpu.VMEM((tokens, count), BF16), pltpu.VMEM((tokens, block), BF16)],
        compiler_params=params(),
        cost_estimate=cost(2 * tokens * count * channels, 2 * count * channels + 8 * tokens * channels),
        name="settle_query",
    )(sources, own, rows, *pieces, *after)


def final_products(shared, a, b, after, name):
    shards, tokens, width = shared.shape
    _, parts, block, steps = column_plan(a.shape[1], shards, 1024)
    return pl.pallas_call(
        final_kernel,
        grid=(steps,),
        in_specs=[
            pl.BlockSpec((parts, tokens, width), lambda j: (j, 0, 0)),
            column(tokens, block), column(tokens, block), UNREAD,
        ],
        out_specs=[column(tokens, block)] * 2,
        out_shape=[shape_of(a.shape, BF16)] * 2,
        compiler_params=params(),
        cost_estimate=cost(2 * a.size, 10 * a.size),
        name=name,
    )(shared, a, b, after)


def permuted(pieces, numbers):
    return [pieces[0]] + [
        lax.ppermute(piece, "ctx", [(i, i ^ number) for i in range(len(pieces))])
        for piece, number in zip(pieces[1:], numbers[1:])
    ]


def exchange(value):
    return lax.all_to_all(value, "ctx", split_axis=0, concat_axis=0, tiled=True)


def per_device(query_rows, key_rows, value_rows, positions, filters, bias_term, grad_out):
    shards = lax.axis_size("ctx")
    ctx_index = lax.axis_index("ctx")
    slots, channels = query_rows.shape
    slot_rows = slots // shards
    tokens = filters.shape[1] // shards
    tables = dense_tables(shards, tokens)

    tensor = lax.axis_size("tp")
    tensor_index = lax.axis_index("tp")
    turn = ctx_index.astype(jnp.int32).reshape(1)
    bias = bias_term.reshape(1, -1)

    query_recv = exchange(query_rows)

    pieces = []
    for shift in range(tensor):
        target = (tensor_index + shift) % tensor
        piece = lax.dynamic_slice_in_dim(grad_out, target * channels, channels, 1)
        if shift:
            piece = lax.ppermute(piece, "tp", [(i, (i + shift) % tensor) for i in range(tensor)])
        pieces.append(piece)
    grad_sources = (tensor_index - jnp.arange(tensor, dtype=jnp.int32)) % tensor

    both_packed = pack(turn, [key_rows, value_rows], shards)
    both_slots = permuted(both_packed, travel_order(shards))
    own = lax.dynamic_slice_in_dim(positions, ctx_index * slot_rows, slot_rows, 1)
    own_turned = jnp.concatenate(
        [lax.dynamic_slice_in_dim(own, ctx_index ^ number, 1, 0) for number in travel_order(shards)],
        axis=1,
    )

    grad_seq, query_seq, grad_conv = settle_query(
        own.reshape(1, slots), query_recv, grad_sources, pieces, tokens, shards, [both_packed[0]]
    )
    grad_recv = exchange(grad_conv)
    filter_spec = filter_spectrum(filters, tables, grad_conv)
    grad_signal, grad_spec = convolve(
        turn, [grad_recv], bias, filter_spec, tables, True, filter_spec
    )
    n_pieces = shards if (channels // shards) % 128 == 0 else 1
    key_seq, value_seq, signal = settle_signal(
        turn, own_turned, both_slots, tokens, n_pieces, grad_signal
    )
    signal_recv = permuted(signal, list(range(shards))) if n_pieces > 1 else [exchange(signal[0])]
    grad_signal = gate(grad_signal, signal_recv)
    grad_signal_recv = exchange(grad_signal)
    conv_out, signal_spec = convolve(
        turn, signal_recv, bias, filter_spec, tables, False, grad_signal
    )
    conv_recv = exchange(conv_out)
    grad_filters = correlate(grad_spec, signal_spec, tables)
    grad_key, grad_value = final_products(
        grad_signal_recv, value_seq, key_seq, grad_filters, "key_value_gradients"
    )
    output, grad_query = final_products(
        conv_recv, query_seq, grad_seq, grad_key, "output_and_query_gradient"
    )
    return output, grad_query, grad_key, grad_value, grad_filters


def solution(mesh):
    return jax.shard_map(
        per_device,
        mesh=mesh,
        in_specs=(
            P("ctx", "tp"),
            P("ctx", "tp"),
            P("ctx", "tp"),
            P(),
            P(("tp", "ctx"), None),
            P(("tp", "ctx")),
            P(("ctx", "tp"), None),
        ),
        out_specs=(
            P("ctx", "tp"),
            P("ctx", "tp"),
            P("ctx", "tp"),
            P("ctx", "tp"),
            P(("tp", "ctx"), None),
        ),
        check_vma=False,
    )
```
